32 devices in a mesh: section: 4 (over y, core), dp: 4 (over z), tensor: 2 (over x).
Axes of the slice: x: 2, y: 2, z: 4, core: 2. Of those that a mesh axis runs over, the one named last changes fastest.
Arguments:
- out_grad: bfloat16 [512, 4096], P('dp', 'tensor'), may hold values from -6 to 6
- section_out: bfloat16 [4, 512, 4096], P('section', 'dp', 'tensor'), may hold values from -6 to 6
- context: bfloat16 [4, 512, 2048], P('section', 'dp', 'tensor'), may hold values from -6 to 6
- queries: bfloat16 [4, 512, 2048], P('section', 'dp', 'tensor')
- key_heads: bfloat16 [4, 512, 2048], P('section', 'dp', 'tensor')
- values: bfloat16 [4, 512, 2048], P('section', 'dp', 'tensor'), may hold values from -6 to 6
- o_weight: bfloat16 [4, 4096, 2048], P('section', None, 'tensor'), may hold values from -0.125 to 0.125
- doc_lengths: int32 [4], replicated, may hold values from 1 to 256, 512 in all
Outputs:
- query_grad: bfloat16 [4, 512, 2048], P('section', 'dp', 'tensor')
- key_grad: bfloat16 [4, 512, 2048], P('section', 'dp', 'tensor')
- value_grad: bfloat16 [4, 512, 2048], P('section', 'dp', 'tensor')
- o_weight_grad: float32 [4, 4096, 2048], P('section', 'dp', 'tensor')
The draws below stay inside these ranges and needn't reach their ends.
Inputs may be any that keep to these rules, and one draw needn't show every extreme that they name: `doc_lengths`: the lengths sum to 512, and the longest document has exactly 256 patches.
All inputs are finite; a program needn't handle non-finite values.
Results may differ from the reference program's by a relative error of at most 0.023.
Values may be sent and summed in bfloat16 or wider, within the bound.
A program may use at most 64 MiB of HBM per device.

```python
import math
import jax
import jax.numpy as jnp
import numpy as np
from jax import lax

D = 4096
HEADS = 16
HD = 128
ROWS = 128
REACH = 2
MOST = 256
DOCS = 4
SECTIONS = 4
ROWS_ALL = 512
WIDE = 2048
N_DP = 4


def queries_and_keys(key):
    seeded = jax.random.fold_in(key, 4242)
    first, second = jax.random.split(seeded, 2)
    full_shape = (SECTIONS, ROWS_ALL, HEADS, HD)
    key_draw = jax.random.normal(first, full_shape, jnp.float32)
    query_draw = jax.random.normal(second, full_shape, jnp.float32)
    flat_shape = (SECTIONS, ROWS_ALL, HEADS * HD)
    return (query_draw.reshape(flat_shape), key_draw.reshape(flat_shape))


def draw_queries(key, part):
    return queries_and_keys(key)[0].astype(jnp.bfloat16)


def draw_key_heads(key, part):
    return queries_and_keys(key)[1].astype(jnp.bfloat16)


def raised(entries, own_key, source, target, shards_of, factor):
    owner, partner = [(jnp.arange(entries.shape[dim]) // (entries.shape[dim] // shards_of)).reshape([-1 if axis == dim else 1 for axis in range(entries.ndim)]) for dim in (source, target)]
    chosen = jax.random.permutation(own_key, shards_of)[partner]
    strong = (owner == chosen) | (owner == (partner + shards_of // 2) % shards_of)
    return jnp.where(strong, factor * entries, entries)


def shard_levels(key, dims, cuts, smallest, high):
    factor_of = 1.0
    for axis_at, blocks in cuts:
        draws = jax.random.uniform(jax.random.fold_in(jax.random.fold_in(key, 6), axis_at), (blocks,), jnp.float32, smallest / len(cuts), high / len(cuts))
        factor_of = factor_of * jnp.repeat(jnp.exp(draws), dims[axis_at] // blocks).reshape((-1,) + (1,) * (len(dims) - 1 - axis_at))
    return factor_of


def profile(number_of, total, limit, skew):
    portions = [(1 << 20) // math.isqrt(rank ** skew) + 1 for rank in range(2, number_of + 1)]
    rest, given = total - limit - (number_of - 1), [1] * (number_of - 1)
    while rest > 0:
        candidates = [i for i in range(number_of - 1) if given[i] < limit]
        whole, budget = sum([portions[i] for i in candidates]), rest
        for i in candidates:
            extra = min(limit - given[i], max(1, budget * portions[i] // whole), rest)
            given[i] = given[i] + extra
            rest = rest - extra
    return np.array([limit] + given)


def uneven_parts(key, number_of, total, limit, lean):
    if number_of == 2:
        one = jax.random.randint(key, (), max(1, total - limit), min(limit, total - 1) + 1)
        return jnp.stack([one, total - one])
    tallies = jnp.asarray(profile(number_of, total, limit, lean), jnp.int32)
    pairs = (number_of - 1) // 2
    donor, taker = tallies[1:1 + 2 * pairs:2], tallies[2:2 + 2 * pairs:2]
    margin = jnp.minimum(donor - 1, limit - taker)
    shifted = jax.random.randint(jax.random.fold_in(key, 1), (pairs,), 0, 1 << 20) % (margin + 1)
    tallies = tallies.at[1:1 + 2 * pairs:2].set(donor - shifted).at[2:2 + 2 * pairs:2].set(taker + shifted)
    return tallies[jax.random.permutation(jax.random.fold_in(key, 2), number_of)]


def noise(key, extent, spread, limit, shards=(), kind=jnp.bfloat16):
    level = shard_levels(key, extent, shards, -0.22, 0.18) if shards else 1.0
    result = jax.random.normal(key, extent, jnp.float32) * spread * level
    return jnp.minimum(jnp.maximum(result, -limit), limit).astype(kind)


def noise_with(own_key, shape, width, bound, cuts, heavy, kind=jnp.bfloat16):
    entries = width * jax.random.normal(own_key, shape, jnp.float32)
    if cuts:
        entries = entries * shard_levels(own_key, shape, cuts, -0.22, 0.18)
    return jnp.clip(raised(entries, jax.random.fold_in(own_key, 3), *heavy), -bound, bound).astype(kind)


def setup_inputs(seed: int = 0) -> dict:
    splits = jax.random.split(jax.random.key(seed), 9)
    out_grad = noise_with(splits[0], (ROWS_ALL, D), 1.0, 6.0, ((0, 4), (1, 2)), (0, 1, 4, 2.0))
    section_out = noise(splits[1], (SECTIONS, ROWS_ALL, D), 1.0, 6.0, ((0, 4), (1, 4), (2, 2)))
    context = noise(splits[2], (SECTIONS, ROWS_ALL, WIDE), 1.0, 6.0, ((0, 4), (1, 4), (2, 2)))
    queries = draw_queries(jax.random.fold_in(splits[8], 71), 0)
    key_heads = draw_key_heads(jax.random.fold_in(splits[8], 71), 0)
    values = noise(splits[5], (SECTIONS, ROWS_ALL, WIDE), 1.0, 6.0, ((0, 4), (1, 4), (2, 2)))
    o_weight = noise(splits[6], (SECTIONS, D, WIDE), WIDE ** -0.5, 0.125, ((0, 4), (2, 2)))
    doc_lengths = uneven_parts(splits[7], DOCS, ROWS_ALL, MOST, 2).astype(jnp.int32)
    return {"out_grad": out_grad, "section_out": section_out, "context": context, "queries": queries, "key_heads": key_heads, "values": values, "o_weight": o_weight, "doc_lengths": doc_lengths}


def rounded(value):
    return lax.optimization_barrier(value.astype(jnp.bfloat16))


def document_of(positions, ends):
    return jnp.sum((positions[:, None] >= ends[None, :]).astype(jnp.int32), axis=-1)


def one_section(out_grad, ends, inputs):
    upper, context, queries, key_heads, values, o_weight = inputs
    scaling = HD ** -0.5
    grad_rows = rounded(out_grad.astype(jnp.float32) + 0.25 * upper)
    d_context = rounded(jnp.dot(grad_rows, o_weight, preferred_element_type=jnp.float32))
    window = (REACH + 1) * ROWS
    front = REACH * ROWS
    three = (ROWS_ALL, HEADS, HD)
    padded_shape = (ROWS_ALL + front, HEADS, HD)
    dctx_f = d_context.astype(jnp.float32).reshape(three)
    ctx_f = context.astype(jnp.float32).reshape(three)
    query_f = queries.astype(jnp.float32).reshape(three)
    blank = jnp.zeros((front, WIDE), jnp.float32)
    key_pad = jnp.concatenate([blank, key_heads.astype(jnp.float32)], 0).reshape(padded_shape)
    value_pad = jnp.concatenate([blank, values.astype(jnp.float32)], 0).reshape(padded_shape)
    places = jnp.arange(ROWS, dtype=jnp.int32)
    spots = jnp.arange(window, dtype=jnp.int32)

    def block(carry, index):
        key_acc, value_acc = carry
        start = (index * ROWS).astype(jnp.int32)
        query_place = start + places
        key_place = start - front + spots
        allowed = (document_of(query_place, ends)[:, None] == document_of(key_place, ends)[None, :])
        allowed = allowed & (key_place[None, :] <= query_place[:, None]) & (key_place[None, :] >= 0)
        query_blk = lax.dynamic_slice_in_dim(query_f, start, ROWS, 0)
        dctx_blk = lax.dynamic_slice_in_dim(dctx_f, start, ROWS, 0)
        ctx_blk = lax.dynamic_slice_in_dim(ctx_f, start, ROWS, 0)
        key_win = lax.dynamic_slice_in_dim(key_pad, start, window, 0)
        value_win = lax.dynamic_slice_in_dim(value_pad, start, window, 0)
        scores = jnp.einsum("ihd,jhd->hij", query_blk, key_win) * scaling
        scores = jnp.where(allowed[None], scores, -jnp.inf)
        prob = jax.nn.softmax(scores, axis=-1)
        prob_b = rounded(prob).astype(jnp.float32)
        d_prob = jnp.einsum("ihd,jhd->hij", dctx_blk, value_win)
        delta = jnp.transpose(jnp.sum(dctx_blk * ctx_blk, axis=-1))
        d_score = rounded(prob * (d_prob - delta[..., None]) * scaling).astype(jnp.float32)
        query_out = jnp.einsum("hij,jhd->ihd", d_score, key_win).astype(jnp.bfloat16)
        key_part = jnp.einsum("hij,ihd->jhd", d_score, query_blk)
        value_part = jnp.einsum("hij,ihd->jhd", prob_b, dctx_blk)
        key_acc = lax.dynamic_update_slice_in_dim(key_acc, lax.dynamic_slice_in_dim(key_acc, start, window, 0) + key_part, start, 0)
        value_acc = lax.dynamic_update_slice_in_dim(value_acc, lax.dynamic_slice_in_dim(value_acc, start, window, 0) + value_part, start, 0)
        return (key_acc, value_acc), query_out

    zeros = jnp.zeros(padded_shape, jnp.float32)
    sums, query_blocks = lax.scan(block, (zeros, zeros), jnp.arange(N_DP, dtype=jnp.int32))
    query_grad = query_blocks.reshape(ROWS_ALL, WIDE)
    key_grad = sums[0][front:].reshape(ROWS_ALL, WIDE).astype(jnp.bfloat16)
    value_grad = sums[1][front:].reshape(ROWS_ALL, WIDE).astype(jnp.bfloat16)
    grad_blocks = grad_rows.reshape(N_DP, ROWS, D)
    ctx_blocks = context.reshape(N_DP, ROWS, WIDE)

    def add_block(index, total):
        grad_part = lax.dynamic_index_in_dim(grad_blocks, index, 0, keepdims=False)
        ctx_part = lax.dynamic_index_in_dim(ctx_blocks, index, 0, keepdims=False)
        term = jnp.dot(grad_part.T, ctx_part, preferred_element_type=jnp.float32)
        return total + rounded(term).astype(jnp.float32)

    weight_grad = lax.fori_loop(0, N_DP, add_block, jnp.zeros((D, WIDE), jnp.float32))
    return (query_grad, key_grad, value_grad, weight_grad)


def reference(out_grad, section_out, context, queries, key_heads, values, o_weight, doc_lengths):
    section_f = section_out.astype(jnp.float32)
    upper = jnp.flip(jnp.cumsum(jnp.flip(section_f, 0), axis=0), 0)
    ends = jnp.cumsum(doc_lengths).astype(jnp.int32)
    results = lax.map(lambda inputs: one_section(out_grad, ends, inputs), (upper, context, queries, key_heads, values, o_weight))
    return (results[0], results[1], results[2], results[3])
```

```python
import jax
import jax.numpy as jnp
from jax import lax
from jax.sharding import PartitionSpec as P

HD = 128
REACH = 2


def passed_along(value, axis, steps):
    count = lax.axis_size(axis)
    leading, last = (max(0, -steps), min(count, count - steps))
    return lax.ppermute(value, axis, [(source, source + steps) for source in range(leading, last)])


def suffix_sum(own, axis):
    count = lax.axis_size(axis)
    total = own.astype(jnp.float32)
    step = 1
    while step < count:
        total = total + passed_along(total.astype(jnp.bfloat16), axis, -step).astype(jnp.float32)
        step *= 2
    return total


def document_of(positions, ends):
    return jnp.sum((positions[:, None] >= ends[None, :]).astype(jnp.int32), axis=-1)


def on_device(out_grad, section_out, context, queries, key_heads, values, o_weight, doc_lengths):
    rows, width = (queries.shape[1], queries.shape[2])
    head_count = width // HD
    scaling = HD ** (-0.5)
    n_dp, n_tensor = lax.axis_size("dp"), lax.axis_size("tensor")
    dp_at, tensor_at = lax.axis_index("dp"), lax.axis_index("tensor")
    docs = doc_lengths.shape[0]
    ends = jnp.sum(
        jnp.where(jnp.arange(docs)[:, None] >= jnp.arange(docs)[None, :], doc_lengths[None, :], 0),
        axis=1,
    )
    three = (rows, head_count, HD)
    first = dp_at * rows
    own_place = first + jnp.arange(rows, dtype=jnp.int32)
    own_docs = document_of(own_place, ends)
    window = (REACH + 1) * rows

    upper = suffix_sum(section_out[0], "section")
    grad_local = (out_grad.astype(jnp.float32) + 0.25 * upper).astype(jnp.bfloat16)

    kv = jnp.concatenate([key_heads[0], values[0]], 1)
    kv_sets, query_flat = [kv], [queries[0]]
    for step in range(REACH):
        kv_sets.append(passed_along(kv_sets[-1], "dp", 1))
        query_flat.append(passed_along(query_flat[-1], "dp", -1))
    context_all = lax.all_gather(context[0], "dp", axis=0, tiled=True)

    local_width = grad_local.shape[1]
    grad_full = jnp.zeros((rows, local_width * n_tensor), jnp.bfloat16)
    d_context = jnp.zeros((rows, width), jnp.float32)
    for step in range(n_tensor):
        part = grad_local
        if step:
            part = lax.ppermute(
                grad_local, "tensor", [(i, (i + step) % n_tensor) for i in range(n_tensor)]
            )
        start = lax.rem(tensor_at + n_tensor - step, n_tensor) * local_width
        grad_full = lax.dynamic_update_slice_in_dim(grad_full, part, start, 1)
        weight = lax.dynamic_slice_in_dim(o_weight[0], start, local_width, 0)
        d_context = d_context + jnp.dot(part, weight, preferred_element_type=jnp.float32)
    d_context = d_context.astype(jnp.bfloat16)
    dctx_flat = [d_context]
    for step in range(REACH):
        dctx_flat.append(passed_along(dctx_flat[-1], "dp", -1))
    grad_blocks = lax.all_to_all(grad_full, "dp", split_axis=1, concat_axis=0, tiled=True)

    query_b = queries[0].reshape(three)
    key_b = key_heads[0].reshape(three)
    value_b = values[0].reshape(three)
    dctx_b = d_context.reshape(three)
    kv_win = jnp.concatenate(kv_sets[::-1], 0)
    key_win = kv_win[:, :width].reshape(window, head_count, HD)
    value_win = kv_win[:, width:].reshape(window, head_count, HD)
    window_place = first - REACH * rows + jnp.arange(window, dtype=jnp.int32)
    window_docs = document_of(window_place, ends)
    allowed = (
        (own_docs[:, None] == window_docs[None, :])
        & (window_place[None, :] <= own_place[:, None])
        & (window_place[None, :] >= 0)
    )
    scores = (
        jnp.einsum("ihd,jhd->hij", query_b, key_win, preferred_element_type=jnp.float32) * scaling
    )
    scores = jnp.where(allowed[None], scores, -jnp.inf)
    peak = jnp.max(scores, axis=-1)
    log_total = peak + jnp.log(jnp.sum(jnp.exp(scores - peak[..., None]), axis=-1))
    total_sets = [log_total]
    for step in range(REACH):
        total_sets.append(passed_along(total_sets[-1], "dp", -1))
    prob = jnp.exp(scores - log_total[..., None])
    d_prob = jnp.einsum("ihd,jhd->hij", dctx_b, value_win, preferred_element_type=jnp.float32)

    dctx_set = jnp.concatenate(dctx_flat, 0).reshape(window, head_count, HD)
    padded = jnp.concatenate([context_all, jnp.zeros((REACH * rows, width), context_all.dtype)], 0)
    context_set = lax.dynamic_slice_in_dim(padded, first, window, 0)
    delta_set = jnp.transpose(
        jnp.sum(
            dctx_set.astype(jnp.float32)
            * context_set.reshape(window, head_count, HD).astype(jnp.float32),
            axis=-1,
        )
    )
    delta = jnp.transpose(
        jnp.sum(dctx_b.astype(jnp.float32) * context[0].reshape(three).astype(jnp.float32), axis=-1)
    )
    d_score = (prob * (d_prob - delta[..., None]) * scaling).astype(jnp.bfloat16)
    query_grad = jnp.einsum(
        "hij,jhd->ihd", d_score, key_win, preferred_element_type=jnp.float32
    ).astype(jnp.bfloat16)

    query_set = jnp.concatenate(query_flat, 0).reshape(window, head_count, HD)
    total_set = jnp.concatenate(total_sets, 1)
    set_place = first + jnp.arange(window, dtype=jnp.int32)
    set_docs = document_of(set_place, ends)
    allowed_back = (
        (set_docs[:, None] == own_docs[None, :])
        & (own_place[None, :] <= set_place[:, None])
        & (set_place[:, None] < n_dp * rows)
    )
    back_scores = (
        jnp.einsum("ihd,jhd->hij", query_set, key_b, preferred_element_type=jnp.float32) * scaling
    )
    prob_back = jnp.exp(jnp.where(allowed_back[None], back_scores - total_set[..., None], -jnp.inf))
    d_prob_back = jnp.einsum("ihd,jhd->hij", dctx_set, value_b, preferred_element_type=jnp.float32)
    d_score_back = (prob_back * (d_prob_back - delta_set[..., None]) * scaling).astype(jnp.bfloat16)
    key_sum = jnp.einsum(
        "hij,ihd->jhd", d_score_back, query_set, preferred_element_type=jnp.float32
    )
    value_sum = jnp.einsum(
        "hij,ihd->jhd",
        prob_back.astype(jnp.bfloat16),
        dctx_set,
        preferred_element_type=jnp.float32,
    )
    weight_grad = lax.dot_general(
        grad_blocks, context_all, (((0,), (0,)), ((), ())), preferred_element_type=jnp.float32
    )
    shape_out = (1, rows, width)
    return (
        query_grad.reshape(shape_out),
        key_sum.astype(jnp.bfloat16).reshape(shape_out),
        value_sum.astype(jnp.bfloat16).reshape(shape_out),
        weight_grad[None],
    )


def solution(mesh):
    placed = (
        P("dp", "tensor"),
        P("section", "dp", "tensor"),
        P("section", "dp", "tensor"),
        P("section", "dp", "tensor"),
        P("section", "dp", "tensor"),
        P("section", "dp", "tensor"),
        P("section", None, "tensor"),
        P(),
    )
    return jax.shard_map(
        on_device,
        mesh=mesh,
        in_specs=placed,
        out_specs=(
            P("section", "dp", "tensor"),
            P("section", "dp", "tensor"),
            P("section", "dp", "tensor"),
            P("section", "dp", "tensor"),
        ),
        check_vma=False,
    )
```

```python
import jax
import jax.numpy as jnp
from jax import lax
from jax.experimental import pallas as pl
from jax.experimental.pallas import tpu as pltpu
from jax.sharding import PartitionSpec as P

HD = 128
REACH = 2


def passed_along(value, axis, steps):
    count = lax.axis_size(axis)
    leading, last = (max(0, -steps), min(count, count - steps))
    return lax.ppermute(value, axis, [(source, source + steps) for source in range(leading, last)])


def suffix_sum(own, axis):
    count = lax.axis_size(axis)
    total = own.astype(jnp.float32)
    step = 1
    while step < count:
        total = total + passed_along(total.astype(jnp.bfloat16), axis, -step).astype(jnp.float32)
        step *= 2
    return total


def document_of(positions, ends):
    return jnp.sum((positions[:, None] >= ends[None, :]).astype(jnp.int32), axis=-1)


def nt(a, b):
    return lax.dot_general(a, b, (((1,), (1,)), ((), ())), preferred_element_type=jnp.float32)


def tn(a, b):
    return lax.dot_general(a, b, (((0,), (0,)), ((), ())), preferred_element_type=jnp.float32)


def head_columns(head, offset=0):
    return slice(offset + head * HD, offset + (head + 1) * HD)


def stacked(refs, columns):
    return jnp.concatenate([ref[:, columns] for ref in refs], 0)


def delta_row(d_context, context):
    product = d_context.astype(jnp.float32) * context.astype(jnp.float32)
    return jnp.sum(jnp.transpose(product), axis=0, keepdims=True)


def totals_kernel(mask_ref, query_ref, *refs):
    kv_refs, total_ref = refs[:-1], refs[-1]
    allowed = mask_ref[...] > 0.0
    for head in range(query_ref.shape[1] // HD):
        columns = head_columns(head)
        scores = nt(stacked(kv_refs, columns), query_ref[:, columns]) * HD ** (-0.5)
        scores = jnp.where(allowed, scores, -jnp.inf)
        peak = jnp.max(scores, axis=0, keepdims=True)
        total = jnp.sum(jnp.exp(scores - peak), axis=0, keepdims=True)
        total_ref[head : head + 1, :] = peak + jnp.log(total)


def query_kernel(mask_ref, query_ref, dctx_ref, context_ref, total_ref, *refs):
    kv_refs, out_ref = refs[:-1], refs[-1]
    scaling = HD ** (-0.5)
    width = query_ref.shape[1]
    allowed = mask_ref[...] > 0.0
    for head in range(width // HD):
        columns = head_columns(head)
        keys = stacked(kv_refs, columns)
        d_context = dctx_ref[:, columns]
        scores = nt(keys, query_ref[:, columns]) * scaling
        prob = jnp.exp(jnp.where(allowed, scores - total_ref[head : head + 1, :], -jnp.inf))
        d_prob = nt(stacked(kv_refs, head_columns(head, width)), d_context)
        delta = delta_row(d_context, context_ref[:, columns])
        d_score = (prob * (d_prob - delta) * scaling).astype(jnp.bfloat16)
        out_ref[:, columns] = tn(d_score, keys).astype(out_ref.dtype)


def key_kernel(sets, mask_ref, key_ref, value_ref, total_ref, *refs):
    query_refs, dctx_refs = refs[:sets], refs[sets : 2 * sets]
    context_refs = refs[2 * sets : 3 * sets]
    key_out, value_out = refs[3 * sets :]
    scaling = HD ** (-0.5)
    allowed = mask_ref[...] > 0.0
    for head in range(key_ref.shape[1] // HD):
        columns = head_columns(head)
        queries = stacked(query_refs, columns)
        d_context = stacked(dctx_refs, columns)
        scores = nt(key_ref[:, columns], queries) * scaling
        prob = jnp.exp(jnp.where(allowed, scores - total_ref[head : head + 1, :], -jnp.inf))
        d_prob = nt(value_ref[:, columns], d_context)
        delta = jnp.concatenate(
            [delta_row(d[:, columns], c[:, columns]) for d, c in zip(dctx_refs, context_refs)], 1
        )
        d_score = (prob * (d_prob - delta) * scaling).astype(jnp.bfloat16)
        key_out[:, columns] = jnp.dot(
            d_score, queries, preferred_element_type=jnp.float32
        ).astype(key_out.dtype)
        value_out[:, columns] = jnp.dot(
            prob.astype(jnp.bfloat16), d_context, preferred_element_type=jnp.float32
        ).astype(value_out.dtype)


def local_kernel(body, shapes, operands, flops):
    whole = pl.BlockSpec(memory_space=pltpu.VMEM)
    moved = sum(a.size * a.dtype.itemsize for a in (*operands, *shapes))
    return pl.pallas_call(
        body,
        out_shape=shapes,
        in_specs=[whole] * len(operands),
        out_specs=[whole] * len(shapes),
        compiler_params=pltpu.CompilerParams(vmem_limit_bytes=32 * 1024 * 1024),
        cost_estimate=pl.CostEstimate(flops=flops, bytes_accessed=moved, transcendentals=0),
    )(*operands)


def on_device(out_grad, section_out, context, queries, key_heads, values, o_weight, doc_lengths):
    rows, width = (queries.shape[1], queries.shape[2])
    head_count = width // HD
    n_dp, n_tensor = lax.axis_size("dp"), lax.axis_size("tensor")
    dp_at, tensor_at = lax.axis_index("dp"), lax.axis_index("tensor")
    docs = doc_lengths.shape[0]
    ends = jnp.sum(
        jnp.where(jnp.arange(docs)[:, None] >= jnp.arange(docs)[None, :], doc_lengths[None, :], 0),
        axis=1,
    )
    first = dp_at * rows
    window = (REACH + 1) * rows

    kv = jnp.concatenate([key_heads[0], values[0]], 1)
    kv_sets, query_sets = [kv], [queries[0]]
    kv_sets.append(passed_along(kv, "dp", 1))
    query_sets.append(passed_along(queries[0], "dp", -1))
    upper = suffix_sum(section_out[0], "section")
    grad_local = (out_grad.astype(jnp.float32) + 0.25 * upper).astype(jnp.bfloat16)
    context_all = lax.all_gather(context[0], "dp", axis=0, tiled=True)

    grad_local, kv_on, query_on = lax.optimization_barrier(
        (grad_local, kv_sets[-1], query_sets[-1])
    )
    kv_sets[-1], query_sets[-1] = kv_on, query_on
    for step in range(1, REACH):
        kv_sets.append(passed_along(kv_sets[-1], "dp", 1))
        query_sets.append(passed_along(query_sets[-1], "dp", -1))

    local_width = grad_local.shape[1]
    grad_full = jnp.zeros((rows, local_width * n_tensor), jnp.bfloat16)
    d_context = jnp.zeros((rows, width), jnp.float32)
    for step in range(n_tensor):
        part = grad_local
        if step:
            part = lax.ppermute(
                grad_local, "tensor", [(i, (i + step) % n_tensor) for i in range(n_tensor)]
            )
        start = lax.rem(tensor_at + n_tensor - step, n_tensor) * local_width
        grad_full = lax.dynamic_update_slice_in_dim(grad_full, part, start, 1)
        weight = lax.dynamic_slice_in_dim(o_weight[0], start, local_width, 0)
        d_context = d_context + jnp.dot(part, weight, preferred_element_type=jnp.float32)
    d_context = d_context.astype(jnp.bfloat16)
    dctx_sets = [d_context]
    for step in range(REACH):
        dctx_sets.append(passed_along(dctx_sets[-1], "dp", -1))
    grad_blocks = lax.all_to_all(grad_full, "dp", split_axis=1, concat_axis=0, tiled=True)

    own_place = first + jnp.arange(rows, dtype=jnp.int32)
    own_docs = document_of(own_place, ends)
    window_place = first - REACH * rows + jnp.arange(window, dtype=jnp.int32)
    window_docs = document_of(window_place, ends)
    allowed = (
        (window_docs[:, None] == own_docs[None, :])
        & (window_place[:, None] <= own_place[None, :])
        & (window_place[:, None] >= 0)
    ).astype(jnp.float32)
    work = 2 * window * rows * width
    kv_win = kv_sets[::-1]
    (total,) = local_kernel(
        totals_kernel,
        [jax.ShapeDtypeStruct((head_count, rows), jnp.float32)],
        (allowed, queries[0], *kv_win),
        work,
    )
    total_sets = [total]
    for step in range(REACH):
        total_sets.append(passed_along(total_sets[-1], "dp", -1))
    flat = jax.ShapeDtypeStruct((rows, width), jnp.bfloat16)
    (query_grad,) = local_kernel(
        query_kernel,
        [flat],
        (allowed, queries[0], d_context, context[0], total, *kv_win),
        3 * work,
    )

    set_place = first + jnp.arange(window, dtype=jnp.int32)
    set_docs = document_of(set_place, ends)
    allowed_back = (
        (own_docs[:, None] == set_docs[None, :])
        & (own_place[:, None] <= set_place[None, :])
        & (set_place[None, :] < n_dp * rows)
    ).astype(jnp.float32)
    context_sets = [context[0]]
    for step in range(1, REACH + 1):
        at = jnp.minimum(dp_at + step, n_dp - 1) * rows
        context_sets.append(lax.dynamic_slice_in_dim(context_all, at, rows, 0))
    key_grad, value_grad = local_kernel(
        lambda *refs: key_kernel(REACH + 1, *refs),
        [flat, flat],
        (
            allowed_back,
            key_heads[0],
            values[0],
            jnp.concatenate(total_sets, 1),
            *query_sets,
            *dctx_sets,
            *context_sets,
        ),
        4 * work,
    )
    weight_grad = lax.dot_general(
        grad_blocks, context_all, (((0,), (0,)), ((), ())), preferred_element_type=jnp.float32
    )
    return query_grad[None], key_grad[None], value_grad[None], weight_grad[None]


def solution(mesh):
    placed = (
        P("dp", "tensor"),
        P("section", "dp", "tensor"),
        P("section", "dp", "tensor"),
        P("section", "dp", "tensor"),
        P("section", "dp", "tensor"),
        P("section", "dp", "tensor"),
        P("section", None, "tensor"),
        P(),
    )
    return jax.shard_map(
        on_device,
        mesh=mesh,
        in_specs=placed,
        out_specs=(
            P("section", "dp", "tensor"),
            P("section", "dp", "tensor"),
            P("section", "dp", "tensor"),
            P("section", "dp", "tensor"),
        ),
        check_vma=False,
    )
```

```python
import jax
import jax.numpy as jnp
from jax import lax
from jax.experimental import pallas as pl
from jax.experimental.pallas import tpu as pltpu
from jax.sharding import PartitionSpec as P

HD = 128
REACH = 2


def passed_along(value, axis, steps):
    count = lax.axis_size(axis)
    leading, last = (max(0, -steps), min(count, count - steps))
    return lax.ppermute(value, axis, [(source, source + steps) for source in range(leading, last)])


def suffix_sum(own, axis):
    count = lax.axis_size(axis)
    total = own.astype(jnp.float32)
    step = 1
    while step < count:
        total = total + passed_along(total.astype(jnp.bfloat16), axis, -step).astype(jnp.float32)
        step *= 2
    return total


def document_of(positions, ends):
    return jnp.sum((positions[:, None] >= ends[None, :]).astype(jnp.int32), axis=-1)


def nt(a, b):
    return lax.dot_general(a, b, (((1,), (1,)), ((), ())), preferred_element_type=jnp.float32)


def tn(a, b):
    return lax.dot_general(a, b, (((0,), (0,)), ((), ())), preferred_element_type=jnp.float32)


def head_columns(head, offset=0):
    return slice(offset + head * HD, offset + (head + 1) * HD)


def stacked(refs, columns):
    return jnp.concatenate([ref[:, columns] for ref in refs], 0)


def delta_row(d_context, context):
    product = d_context.astype(jnp.float32) * context.astype(jnp.float32)
    return jnp.sum(jnp.transpose(product), axis=0, keepdims=True)


def totals_kernel(after_ref, mask_ref, query_ref, *refs):
    del after_ref
    kv_refs, total_ref = refs[:-1], refs[-1]
    allowed = mask_ref[...] > 0.0
    for head in range(query_ref.shape[1] // HD):
        columns = head_columns(head)
        scores = nt(stacked(kv_refs, columns), query_ref[:, columns]) * HD ** (-0.5)
        scores = jnp.where(allowed, scores, -jnp.inf)
        peak = jnp.max(scores, axis=0, keepdims=True)
        total = jnp.sum(jnp.exp(scores - peak), axis=0, keepdims=True)
        total_ref[head : head + 1, :] = peak + jnp.log(total)


def query_kernel(mask_ref, query_ref, dctx_ref, context_ref, total_ref, *refs):
    kv_refs, out_ref = refs[:-1], refs[-1]
    scaling = HD ** (-0.5)
    width = query_ref.shape[1]
    allowed = mask_ref[...] > 0.0
    for head in range(width // HD):
        columns = head_columns(head)
        keys = stacked(kv_refs, columns)
        d_context = dctx_ref[:, columns]
        scores = nt(keys, query_ref[:, columns]) * scaling
        prob = jnp.exp(jnp.where(allowed, scores - total_ref[head : head + 1, :], -jnp.inf))
        d_prob = nt(stacked(kv_refs, head_columns(head, width)), d_context)
        delta = delta_row(d_context, context_ref[:, columns])
        d_score = (prob * (d_prob - delta) * scaling).astype(jnp.bfloat16)
        out_ref[:, columns] = tn(d_score, keys).astype(out_ref.dtype)


def key_kernel(sets, mask_ref, key_ref, value_ref, total_ref, *refs):
    query_refs, dctx_refs = refs[:sets], refs[sets : 2 * sets]
    context_refs = refs[2 * sets : 3 * sets]
    key_out, value_out = refs[3 * sets :]
    scaling = HD ** (-0.5)
    allowed = mask_ref[...] > 0.0
    for head in range(key_ref.shape[1] // HD):
        columns = head_columns(head)
        queries = stacked(query_refs, columns)
        d_context = stacked(dctx_refs, columns)
        scores = nt(key_ref[:, columns], queries) * scaling
        prob = jnp.exp(jnp.where(allowed, scores - total_ref[head : head + 1, :], -jnp.inf))
        d_prob = nt(value_ref[:, columns], d_context)
        delta = jnp.concatenate(
            [delta_row(d[:, columns], c[:, columns]) for d, c in zip(dctx_refs, context_refs)], 1
        )
        d_score = (prob * (d_prob - delta) * scaling).astype(jnp.bfloat16)
        key_out[:, columns] = jnp.dot(
            d_score, queries, preferred_element_type=jnp.float32
        ).astype(key_out.dtype)
        value_out[:, columns] = jnp.dot(
            prob.astype(jnp.bfloat16), d_context, preferred_element_type=jnp.float32
        ).astype(value_out.dtype)


def local_kernel(body, shapes, operands, flops):
    whole = pl.BlockSpec(memory_space=pltpu.VMEM)
    moved = sum(a.size * a.dtype.itemsize for a in (*operands, *shapes))
    return pl.pallas_call(
        body,
        out_shape=shapes,
        in_specs=[whole] * len(operands),
        out_specs=[whole] * len(shapes),
        compiler_params=pltpu.CompilerParams(vmem_limit_bytes=32 * 1024 * 1024),
        cost_estimate=pl.CostEstimate(flops=flops, bytes_accessed=moved, transcendentals=0),
    )(*operands)


def on_device(out_grad, section_out, context, queries, key_heads, values, o_weight, doc_lengths):
    rows, width = (queries.shape[1], queries.shape[2])
    head_count = width // HD
    n_dp, n_tensor = lax.axis_size("dp"), lax.axis_size("tensor")
    dp_at, tensor_at = lax.axis_index("dp"), lax.axis_index("tensor")
    docs = doc_lengths.shape[0]
    ends = jnp.sum(
        jnp.where(jnp.arange(docs)[:, None] >= jnp.arange(docs)[None, :], doc_lengths[None, :], 0),
        axis=1,
    )
    first = dp_at * rows
    window = (REACH + 1) * rows

    kv = jnp.concatenate([key_heads[0], values[0]], 1)
    own_out, kv, context_own = lax.optimization_barrier((section_out[0], kv, context[0]))
    kv_sets, query_sets = [kv], [queries[0]]
    for step in range(1, REACH + 1):
        kv_sets.append(passed_along(kv, "dp", step))
        query_sets.append(passed_along(queries[0], "dp", -step))
    upper = suffix_sum(own_out, "section")
    grad_local = (out_grad.astype(jnp.float32) + 0.25 * upper).astype(jnp.bfloat16)
    context_all = lax.all_gather(context_own, "dp", axis=0, tiled=True)

    local_width = grad_local.shape[1]
    grad_full = jnp.zeros((rows, local_width * n_tensor), jnp.bfloat16)
    d_context = jnp.zeros((rows, width), jnp.float32)
    for step in range(n_tensor):
        part = grad_local
        if step:
            part = lax.ppermute(
                grad_local, "tensor", [(i, (i + step) % n_tensor) for i in range(n_tensor)]
            )
        start = lax.rem(tensor_at + n_tensor - step, n_tensor) * local_width
        grad_full = lax.dynamic_update_slice_in_dim(grad_full, part, start, 1)
        weight = lax.dynamic_slice_in_dim(o_weight[0], start, local_width, 0)
        d_context = d_context + jnp.dot(part, weight, preferred_element_type=jnp.float32)
    d_context = d_context.astype(jnp.bfloat16)
    dctx_sets = [d_context]
    for step in range(REACH):
        dctx_sets.append(passed_along(dctx_sets[-1], "dp", -1))
    grad_blocks = lax.all_to_all(grad_full, "dp", split_axis=1, concat_axis=0, tiled=True)

    own_place = first + jnp.arange(rows, dtype=jnp.int32)
    own_docs = document_of(own_place, ends)
    window_place = first - REACH * rows + jnp.arange(window, dtype=jnp.int32)
    window_docs = document_of(window_place, ends)
    allowed = (
        (window_docs[:, None] == own_docs[None, :])
        & (window_place[:, None] <= own_place[None, :])
        & (window_place[:, None] >= 0)
    ).astype(jnp.float32)
    work = 2 * window * rows * width
    kv_win = kv_sets[::-1]
    (total,) = local_kernel(
        totals_kernel,
        [jax.ShapeDtypeStruct((head_count, rows), jnp.float32)],
        (d_context, allowed, queries[0], *kv_win),
        work,
    )
    total_sets = [total]
    for step in range(1, REACH + 1):
        total_sets.append(passed_along(total, "dp", -step))
    flat = jax.ShapeDtypeStruct((rows, width), jnp.bfloat16)
    (query_grad,) = local_kernel(
        query_kernel,
        [flat],
        (allowed, queries[0], d_context, context[0], total, *kv_win),
        3 * work,
    )

    set_place = first + jnp.arange(window, dtype=jnp.int32)
    set_docs = document_of(set_place, ends)
    allowed_back = (
        (own_docs[:, None] == set_docs[None, :])
        & (own_place[:, None] <= set_place[None, :])
        & (set_place[None, :] < n_dp * rows)
    ).astype(jnp.float32)
    context_sets = [context[0]]
    for step in range(1, REACH + 1):
        at = jnp.minimum(dp_at + step, n_dp - 1) * rows
        context_sets.append(lax.dynamic_slice_in_dim(context_all, at, rows, 0))
    key_grad, value_grad = local_kernel(
        lambda *refs: key_kernel(REACH + 1, *refs),
        [flat, flat],
        (
            allowed_back,
            key_heads[0],
            values[0],
            jnp.concatenate(total_sets, 1),
            *query_sets,
            *dctx_sets,
            *context_sets,
        ),
        4 * work,
    )
    weight_grad = lax.dot_general(
        grad_blocks, context_all, (((0,), (0,)), ((), ())), preferred_element_type=jnp.float32
    )
    return query_grad[None], key_grad[None], value_grad[None], weight_grad[None]


def solution(mesh):
    placed = (
        P("dp", "tensor"),
        P("section", "dp", "tensor"),
        P("section", "dp", "tensor"),
        P("section", "dp", "tensor"),
        P("section", "dp", "tensor"),
        P("section", "dp", "tensor"),
        P("section", None, "tensor"),
        P(),
    )
    return jax.shard_map(
        on_device,
        mesh=mesh,
        in_specs=placed,
        out_specs=(
            P("section", "dp", "tensor"),
            P("section", "dp", "tensor"),
            P("section", "dp", "tensor"),
            P("section", "dp", "tensor"),
        ),
        check_vma=False,
    )
```

```python
import jax
import jax.numpy as jnp
from jax import lax
from jax.experimental import pallas as pl
from jax.experimental.pallas import tpu as pltpu
from jax.sharding import PartitionSpec as P

HD = 128
REACH = 2


def passed_along(value, axis, steps):
    count = lax.axis_size(axis)
    leading, last = (max(0, -steps), min(count, count - steps))
    return lax.ppermute(value, axis, [(source, source + steps) for source in range(leading, last)])


def suffix_sum(own, axis):
    count = lax.axis_size(axis)
    total = own.astype(jnp.float32)
    step = 1
    while step < count:
        total = total + passed_along(total.astype(jnp.bfloat16), axis, -step).astype(jnp.float32)
        step *= 2
    return total


def document_of(positions, ends):
    return jnp.sum((positions[:, None] >= ends[None, :]).astype(jnp.int32), axis=-1)


def nt(a, b):
    return lax.dot_general(a, b, (((1,), (1,)), ((), ())), preferred_element_type=jnp.float32)


def tn(a, b):
    return lax.dot_general(a, b, (((0,), (0,)), ((), ())), preferred_element_type=jnp.float32)


def head_columns(head, offset=0):
    return slice(offset + head * HD, offset + (head + 1) * HD)


def stacked(refs, columns):
    return jnp.concatenate([ref[:, columns] for ref in refs], 0)


def delta_row(d_context, context):
    product = d_context.astype(jnp.float32) * context.astype(jnp.float32)
    return jnp.sum(jnp.transpose(product), axis=0, keepdims=True)


def totals_kernel(after_ref, mask_ref, query_ref, *refs):
    del after_ref
    kv_refs, total_ref = refs[:-1], refs[-1]
    allowed = mask_ref[...] > 0.0
    for head in range(query_ref.shape[1] // HD):
        columns = head_columns(head)
        scores = nt(stacked(kv_refs, columns), query_ref[:, columns]) * HD ** (-0.5)
        scores = jnp.where(allowed, scores, -jnp.inf)
        peak = jnp.max(scores, axis=0, keepdims=True)
        total = jnp.sum(jnp.exp(scores - peak), axis=0, keepdims=True)
        total_ref[head : head + 1, :] = peak + jnp.log(total)


def query_kernel(mask_ref, query_ref, dctx_ref, context_ref, total_ref, *refs):
    kv_refs, out_ref = refs[:-1], refs[-1]
    scaling = HD ** (-0.5)
    width = query_ref.shape[1]
    allowed = mask_ref[...] > 0.0
    for head in range(width // HD):
        columns = head_columns(head)
        keys = stacked(kv_refs, columns)
        d_context = dctx_ref[:, columns]
        scores = nt(keys, query_ref[:, columns]) * scaling
        prob = jnp.exp(jnp.where(allowed, scores - total_ref[head : head + 1, :], -jnp.inf))
        d_prob = nt(stacked(kv_refs, head_columns(head, width)), d_context)
        delta = delta_row(d_context, context_ref[:, columns])
        d_score = (prob * (d_prob - delta) * scaling).astype(jnp.bfloat16)
        out_ref[:, columns] = tn(d_score, keys).astype(out_ref.dtype)


def key_kernel(sets, mask_ref, key_ref, value_ref, total_ref, *refs):
    query_refs, dctx_refs = refs[:sets], refs[sets : 2 * sets]
    context_refs = refs[2 * sets : 3 * sets]
    key_out, value_out = refs[3 * sets :]
    scaling = HD ** (-0.5)
    allowed = mask_ref[...] > 0.0
    for head in range(key_ref.shape[1] // HD):
        columns = head_columns(head)
        queries = stacked(query_refs, columns)
        d_context = stacked(dctx_refs, columns)
        scores = nt(key_ref[:, columns], queries) * scaling
        prob = jnp.exp(jnp.where(allowed, scores - total_ref[head : head + 1, :], -jnp.inf))
        d_prob = nt(value_ref[:, columns], d_context)
        delta = jnp.concatenate(
            [delta_row(d[:, columns], c[:, columns]) for d, c in zip(dctx_refs, context_refs)], 1
        )
        d_score = (prob * (d_prob - delta) * scaling).astype(jnp.bfloat16)
        key_out[:, columns] = jnp.dot(
            d_score, queries, preferred_element_type=jnp.float32
        ).astype(key_out.dtype)
        value_out[:, columns] = jnp.dot(
            prob.astype(jnp.bfloat16), d_context, preferred_element_type=jnp.float32
        ).astype(value_out.dtype)


def local_kernel(body, shapes, operands, flops):
    whole = pl.BlockSpec(memory_space=pltpu.VMEM)
    moved = sum(a.size * a.dtype.itemsize for a in (*operands, *shapes))
    return pl.pallas_call(
        body,
        out_shape=shapes,
        in_specs=[whole] * len(operands),
        out_specs=[whole] * len(shapes),
        compiler_params=pltpu.CompilerParams(vmem_limit_bytes=32 * 1024 * 1024),
        cost_estimate=pl.CostEstimate(flops=flops, bytes_accessed=moved, transcendentals=0),
    )(*operands)


def on_device(out_grad, section_out, context, queries, key_heads, values, o_weight, doc_lengths):
    rows, width = (queries.shape[1], queries.shape[2])
    head_count = width // HD
    n_dp, n_tensor = lax.axis_size("dp"), lax.axis_size("tensor")
    dp_at, tensor_at = lax.axis_index("dp"), lax.axis_index("tensor")
    docs = doc_lengths.shape[0]
    ends = jnp.sum(
        jnp.where(jnp.arange(docs)[:, None] >= jnp.arange(docs)[None, :], doc_lengths[None, :], 0),
        axis=1,
    )
    first = dp_at * rows
    window = (REACH + 1) * rows

    kv = jnp.concatenate([key_heads[0], values[0]], 1)
    own_out, kv, context_own = lax.optimization_barrier((section_out[0], kv, context[0]))
    kv_sets, query_sets = [kv], [queries[0]]
    for step in range(1, REACH + 1):
        kv_sets.append(passed_along(kv, "dp", step))
        query_sets.append(passed_along(queries[0], "dp", -step))
    upper = suffix_sum(own_out, "section")
    grad_local = (out_grad.astype(jnp.float32) + 0.25 * upper).astype(jnp.bfloat16)
    context_all = lax.all_gather(context_own, "dp", axis=0, tiled=True)

    local_width = grad_local.shape[1]
    grad_full = jnp.zeros((rows, local_width * n_tensor), jnp.bfloat16)
    d_context = jnp.zeros((rows, width), jnp.float32)
    for step in range(n_tensor):
        part = grad_local
        if step:
            part = lax.ppermute(
                grad_local, "tensor", [(i, (i + step) % n_tensor) for i in range(n_tensor)]
            )
        start = lax.rem(tensor_at + n_tensor - step, n_tensor) * local_width
        grad_full = lax.dynamic_update_slice_in_dim(grad_full, part, start, 1)
        weight = lax.dynamic_slice_in_dim(o_weight[0], start, local_width, 0)
        d_context = d_context + jnp.dot(part, weight, preferred_element_type=jnp.float32)
    d_context = d_context.astype(jnp.bfloat16)
    dctx_sets = [d_context]
    for step in range(REACH):
        dctx_sets.append(passed_along(dctx_sets[-1], "dp", -1))
    block = grad_full.shape[1] // n_dp
    share = block // n_tensor
    grad_share = lax.dynamic_index_in_dim(
        grad_full.reshape(rows, n_dp, n_tensor, share), tensor_at, 2, keepdims=False
    )
    grad_share = lax.all_to_all(
        grad_share.reshape(rows, n_dp * share), "dp", split_axis=1, concat_axis=0, tiled=True
    )

    own_place = first + jnp.arange(rows, dtype=jnp.int32)
    own_docs = document_of(own_place, ends)
    window_place = first - REACH * rows + jnp.arange(window, dtype=jnp.int32)
    window_docs = document_of(window_place, ends)
    allowed = (
        (window_docs[:, None] == own_docs[None, :])
        & (window_place[:, None] <= own_place[None, :])
        & (window_place[:, None] >= 0)
    ).astype(jnp.float32)
    work = 2 * window * rows * width
    kv_win = kv_sets[::-1]
    (total,) = local_kernel(
        totals_kernel,
        [jax.ShapeDtypeStruct((head_count, rows), jnp.float32)],
        (d_context, allowed, queries[0], *kv_win),
        work,
    )
    total_sets = [total]
    for step in range(1, REACH + 1):
        total_sets.append(passed_along(total, "dp", -step))
    flat = jax.ShapeDtypeStruct((rows, width), jnp.bfloat16)
    (query_grad,) = local_kernel(
        query_kernel,
        [flat],
        (allowed, queries[0], d_context, context[0], total, *kv_win),
        3 * work,
    )

    set_place = first + jnp.arange(window, dtype=jnp.int32)
    set_docs = document_of(set_place, ends)
    allowed_back = (
        (own_docs[:, None] == set_docs[None, :])
        & (own_place[:, None] <= set_place[None, :])
        & (set_place[None, :] < n_dp * rows)
    ).astype(jnp.float32)
    context_sets = [context[0]]
    for step in range(1, REACH + 1):
        at = jnp.minimum(dp_at + step, n_dp - 1) * rows
        context_sets.append(lax.dynamic_slice_in_dim(context_all, at, rows, 0))
    key_grad, value_grad = local_kernel(
        lambda *refs: key_kernel(REACH + 1, *refs),
        [flat, flat],
        (
            allowed_back,
            key_heads[0],
            values[0],
            jnp.concatenate(total_sets, 1),
            *query_sets,
            *dctx_sets,
            *context_sets,
        ),
        4 * work,
    )
    grad_blocks = jnp.zeros((n_dp * rows, block), jnp.bfloat16)
    for step in range(n_tensor):
        part = grad_share
        if step:
            part = lax.ppermute(
                grad_share, "tensor", [(i, (i + step) % n_tensor) for i in range(n_tensor)]
            )
        start = lax.rem(tensor_at + n_tensor - step, n_tensor) * share
        grad_blocks = lax.dynamic_update_slice_in_dim(grad_blocks, part, start, 1)
    weight_grad = lax.dot_general(
        grad_blocks, context_all, (((0,), (0,)), ((), ())), preferred_element_type=jnp.float32
    )
    return query_grad[None], key_grad[None], value_grad[None], weight_grad[None]


def solution(mesh):
    placed = (
        P("dp", "tensor"),
        P("section", "dp", "tensor"),
        P("section", "dp", "tensor"),
        P("section", "dp", "tensor"),
        P("section", "dp", "tensor"),
        P("section", "dp", "tensor"),
        P("section", None, "tensor"),
        P(),
    )
    return jax.shard_map(
        on_device,
        mesh=mesh,
        in_specs=placed,
        out_specs=(
            P("section", "dp", "tensor"),
            P("section", "dp", "tensor"),
            P("section", "dp", "tensor"),
            P("section", "dp", "tensor"),
        ),
        check_vma=False,
    )
```

```python
import jax
import jax.numpy as jnp
from jax import lax
from jax.experimental import pallas as pl
from jax.experimental.pallas import tpu as pltpu
from jax.sharding import PartitionSpec as P

HD = 128
REACH = 2


def passed_along(value, axis, steps):
    count = lax.axis_size(axis)
    leading, last = (max(0, -steps), min(count, count - steps))
    return lax.ppermute(value, axis, [(source, source + steps) for source in range(leading, last)])


def suffix_sum(own, axis):
    count = lax.axis_size(axis)
    total = own.astype(jnp.float32)
    step = 1
    while step < count:
        total = total + passed_along(total.astype(jnp.bfloat16), axis, -step).astype(jnp.float32)
        step *= 2
    return total


def document_of(positions, ends):
    return jnp.sum((positions[:, None] >= ends[None, :]).astype(jnp.int32), axis=-1)


def nt(a, b):
    return lax.dot_general(a, b, (((1,), (1,)), ((), ())), preferred_element_type=jnp.float32)


def tn(a, b):
    return lax.dot_general(a, b, (((0,), (0,)), ((), ())), preferred_element_type=jnp.float32)


def head_columns(head, offset=0):
    return slice(offset + head * HD, offset + (head + 1) * HD)


def stacked(refs, columns):
    return jnp.concatenate([ref[:, columns] for ref in refs], 0)


def delta_row(d_context, context):
    product = d_context.astype(jnp.float32) * context.astype(jnp.float32)
    return jnp.sum(jnp.transpose(product), axis=0, keepdims=True)


def totals_kernel(ahead, *refs):
    mask_ref, query_ref, *refs = refs[ahead:]
    kv_refs, total_ref = refs[:-1], refs[-1]
    allowed = mask_ref[...] > 0.0
    for head in range(query_ref.shape[1] // HD):
        columns = head_columns(head)
        scores = nt(stacked(kv_refs, columns), query_ref[:, columns]) * HD ** (-0.5)
        scores = jnp.where(allowed, scores, -jnp.inf)
        peak = jnp.max(scores, axis=0, keepdims=True)
        total = jnp.sum(jnp.exp(scores - peak), axis=0, keepdims=True)
        total_ref[head : head + 1, :] = peak + jnp.log(total)


def query_kernel(mask_ref, query_ref, dctx_ref, context_ref, total_ref, *refs):
    kv_refs, out_ref = refs[:-1], refs[-1]
    scaling = HD ** (-0.5)
    width = query_ref.shape[1]
    allowed = mask_ref[...] > 0.0
    for head in range(width // HD):
        columns = head_columns(head)
        keys = stacked(kv_refs, columns)
        d_context = dctx_ref[:, columns]
        scores = nt(keys, query_ref[:, columns]) * scaling
        prob = jnp.exp(jnp.where(allowed, scores - total_ref[head : head + 1, :], -jnp.inf))
        d_prob = nt(stacked(kv_refs, head_columns(head, width)), d_context)
        delta = delta_row(d_context, context_ref[:, columns])
        d_score = (prob * (d_prob - delta) * scaling).astype(jnp.bfloat16)
        out_ref[:, columns] = tn(d_score, keys).astype(out_ref.dtype)


def key_kernel(sets, mask_ref, key_ref, value_ref, total_ref, *refs):
    query_refs, dctx_refs = refs[:sets], refs[sets : 2 * sets]
    context_refs = refs[2 * sets : 3 * sets]
    key_out, value_out = refs[3 * sets :]
    scaling = HD ** (-0.5)
    allowed = mask_ref[...] > 0.0
    for head in range(key_ref.shape[1] // HD):
        columns = head_columns(head)
        queries = stacked(query_refs, columns)
        d_context = stacked(dctx_refs, columns)
        scores = nt(key_ref[:, columns], queries) * scaling
        prob = jnp.exp(jnp.where(allowed, scores - total_ref[head : head + 1, :], -jnp.inf))
        d_prob = nt(value_ref[:, columns], d_context)
        delta = jnp.concatenate(
            [delta_row(d[:, columns], c[:, columns]) for d, c in zip(dctx_refs, context_refs)], 1
        )
        d_score = (prob * (d_prob - delta) * scaling).astype(jnp.bfloat16)
        key_out[:, columns] = jnp.dot(
            d_score, queries, preferred_element_type=jnp.float32
        ).astype(key_out.dtype)
        value_out[:, columns] = jnp.dot(
            prob.astype(jnp.bfloat16), d_context, preferred_element_type=jnp.float32
        ).astype(value_out.dtype)


def local_kernel(body, shapes, operands, flops):
    whole = pl.BlockSpec(memory_space=pltpu.VMEM)
    moved = sum(a.size * a.dtype.itemsize for a in (*operands, *shapes))
    return pl.pallas_call(
        body,
        out_shape=shapes,
        in_specs=[whole] * len(operands),
        out_specs=[whole] * len(shapes),
        compiler_params=pltpu.CompilerParams(vmem_limit_bytes=32 * 1024 * 1024),
        cost_estimate=pl.CostEstimate(flops=flops, bytes_accessed=moved, transcendentals=0),
    )(*operands)


def on_device(out_grad, section_out, context, queries, key_heads, values, o_weight, doc_lengths):
    rows, width = (queries.shape[1], queries.shape[2])
    head_count = width // HD
    n_dp, n_tensor = lax.axis_size("dp"), lax.axis_size("tensor")
    dp_at, tensor_at = lax.axis_index("dp"), lax.axis_index("tensor")
    docs = doc_lengths.shape[0]
    ends = jnp.sum(
        jnp.where(jnp.arange(docs)[:, None] >= jnp.arange(docs)[None, :], doc_lengths[None, :], 0),
        axis=1,
    )
    first = dp_at * rows
    window = (REACH + 1) * rows

    kv = jnp.concatenate([key_heads[0], values[0]], 1)
    own_out, kv, context_own = lax.optimization_barrier((section_out[0], kv, context[0]))
    kv_sets, query_sets = [kv], [queries[0]]
    for step in range(1, REACH + 1):
        kv_sets.append(passed_along(kv, "dp", step))
        query_sets.append(passed_along(queries[0], "dp", -step))
    upper = suffix_sum(own_out, "section")
    grad_local = (out_grad.astype(jnp.float32) + 0.25 * upper).astype(jnp.bfloat16)
    context_all = lax.all_gather(context_own, "dp", axis=0, tiled=True)

    local_width = grad_local.shape[1]
    grad_full = jnp.zeros((rows, local_width * n_tensor), jnp.bfloat16)
    d_context = jnp.zeros((rows, width), jnp.float32)
    for step in range(n_tensor):
        part = grad_local
        if step:
            part = lax.ppermute(
                grad_local, "tensor", [(i, (i + step) % n_tensor) for i in range(n_tensor)]
            )
        start = lax.rem(tensor_at + n_tensor - step, n_tensor) * local_width
        grad_full = lax.dynamic_update_slice_in_dim(grad_full, part, start, 1)
        weight = lax.dynamic_slice_in_dim(o_weight[0], start, local_width, 0)
        d_context = d_context + jnp.dot(part, weight, preferred_element_type=jnp.float32)
    d_context = d_context.astype(jnp.bfloat16)
    dctx_sets = [d_context]
    for step in range(REACH):
        dctx_sets.append(passed_along(dctx_sets[-1], "dp", -1))
    block = grad_full.shape[1] // n_dp
    share = block // n_tensor
    grad_share = lax.dynamic_index_in_dim(
        grad_full.reshape(rows, n_dp, n_tensor, share), tensor_at, 2, keepdims=False
    )
    grad_share = lax.all_to_all(
        grad_share.reshape(rows, n_dp * share), "dp", split_axis=1, concat_axis=0, tiled=True
    )

    own_place = first + jnp.arange(rows, dtype=jnp.int32)
    own_docs = document_of(own_place, ends)
    window_place = first - REACH * rows + jnp.arange(window, dtype=jnp.int32)
    window_docs = document_of(window_place, ends)
    allowed = (
        (window_docs[:, None] == own_docs[None, :])
        & (window_place[:, None] <= own_place[None, :])
        & (window_place[:, None] >= 0)
    ).astype(jnp.float32)
    work = 2 * window * rows * width
    kv_win = kv_sets[::-1]
    (total,) = local_kernel(
        lambda *refs: totals_kernel(REACH + 1, *refs),
        [jax.ShapeDtypeStruct((head_count, rows), jnp.float32)],
        (d_context, *query_sets[1:], allowed, queries[0], *kv_win),
        work,
    )
    total_sets = [total]
    for step in range(1, REACH + 1):
        total_sets.append(passed_along(total, "dp", -step))
    flat = jax.ShapeDtypeStruct((rows, width), jnp.bfloat16)
    (query_grad,) = local_kernel(
        query_kernel,
        [flat],
        (allowed, queries[0], d_context, context[0], total, *kv_win),
        3 * work,
    )

    set_place = first + jnp.arange(window, dtype=jnp.int32)
    set_docs = document_of(set_place, ends)
    allowed_back = (
        (own_docs[:, None] == set_docs[None, :])
        & (own_place[:, None] <= set_place[None, :])
        & (set_place[None, :] < n_dp * rows)
    ).astype(jnp.float32)
    context_sets = [context[0]]
    for step in range(1, REACH + 1):
        at = jnp.minimum(dp_at + step, n_dp - 1) * rows
        context_sets.append(lax.dynamic_slice_in_dim(context_all, at, rows, 0))
    key_grad, value_grad = local_kernel(
        lambda *refs: key_kernel(REACH + 1, *refs),
        [flat, flat],
        (
            allowed_back,
            key_heads[0],
            values[0],
            jnp.concatenate(total_sets, 1),
            *query_sets,
            *dctx_sets,
            *context_sets,
        ),
        4 * work,
    )
    grad_blocks = jnp.zeros((n_dp * rows, block), jnp.bfloat16)
    for step in range(n_tensor):
        part = grad_share
        if step:
            part = lax.ppermute(
                grad_share, "tensor", [(i, (i + step) % n_tensor) for i in range(n_tensor)]
            )
        start = lax.rem(tensor_at + n_tensor - step, n_tensor) * share
        grad_blocks = lax.dynamic_update_slice_in_dim(grad_blocks, part, start, 1)
    weight_grad = lax.dot_general(
        grad_blocks, context_all, (((0,), (0,)), ((), ())), preferred_element_type=jnp.float32
    )
    return query_grad[None], key_grad[None], value_grad[None], weight_grad[None]


def solution(mesh):
    placed = (
        P("dp", "tensor"),
        P("section", "dp", "tensor"),
        P("section", "dp", "tensor"),
        P("section", "dp", "tensor"),
        P("section", "dp", "tensor"),
        P("section", "dp", "tensor"),
        P("section", None, "tensor"),
        P(),
    )
    return jax.shard_map(
        on_device,
        mesh=mesh,
        in_specs=placed,
        out_specs=(
            P("section", "dp", "tensor"),
            P("section", "dp", "tensor"),
            P("section", "dp", "tensor"),
            P("section", "dp", "tensor"),
        ),
        check_vma=False,
    )
```
